32 devices in a mesh: ctx: 8 (over y, x, core), fsdp: 4 (over z).
Axes of the slice: x: 2, y: 2, z: 4, core: 2. Of those that a mesh axis runs over, the one named last changes fastest.
Arguments:
- tokens: bfloat16 [4, 1024, 1024], P('fsdp', 'ctx'), may hold values from -6 to 6
- cotangent: float32 [4, 1024, 1024], P('fsdp', 'ctx'), may hold values from -6 to 6
- block_order: int32 [4, 16], P('fsdp'), may hold values from 0 to 15, each once within a row
- ln1_gain: bfloat16 [1, 1024], P(None, 'fsdp'), may hold values from 0.099609375 to 1.8984375
- ln1_bias: bfloat16 [1, 1024], P(None, 'fsdp'), may hold values from -4 to 4
- qkv_weight: bfloat16 [1, 1024, 3072], P(None, 'fsdp'), may hold values from -0.1875 to 0.1875
- query_bias: bfloat16 [1, 1024], P(None, 'fsdp'), may hold values from -6 to 6
- value_bias: bfloat16 [1, 1024], P(None, 'fsdp'), may hold values from -6 to 6
- proj_weight: bfloat16 [1, 1024, 1024], P(None, 'fsdp'), may hold values from -0.75 to 0.75
- proj_bias: bfloat16 [1, 1024], P(None, 'fsdp'), may hold values from -4 to 4
- ln2_gain: bfloat16 [1, 1024], P(None, 'fsdp'), may hold values from 0.099609375 to 1.8984375
- ln2_bias: bfloat16 [1, 1024], P(None, 'fsdp'), may hold values from -4 to 4
- fc_weight: bfloat16 [1, 1024, 4096], P(None, 'fsdp'), may hold values from -0.1875 to 0.1875
- fc_bias: bfloat16 [1, 4096], P(None, 'fsdp'), may hold values from -6 to 6
- out_weight: bfloat16 [1, 4096, 1024], P(None, 'fsdp'), may hold values from -0.09375 to 0.09375
- out_bias: bfloat16 [1, 1024], P(None, 'fsdp'), may hold values from -4 to 4
Outputs:
- block_out: float32 [4, 1024, 1024], P('fsdp', 'ctx')
- input_grad: float32 [4, 1024, 1024], P('fsdp', 'ctx')
- ln1_gain_grad: float32 [1, 1024], P(None, 'fsdp')
- ln1_bias_grad: float32 [1, 1024], P(None, 'fsdp')
- qkv_weight_grad: float32 [1, 1024, 3072], P(None, 'fsdp')
- query_bias_grad: float32 [1, 1024], P(None, 'fsdp')
- value_bias_grad: float32 [1, 1024], P(None, 'fsdp')
- proj_weight_grad: float32 [1, 1024, 1024], P(None, 'fsdp')
- proj_bias_grad: float32 [1, 1024], P(None, 'fsdp')
- ln2_gain_grad: float32 [1, 1024], P(None, 'fsdp')
- ln2_bias_grad: float32 [1, 1024], P(None, 'fsdp')
- fc_weight_grad: float32 [1, 1024, 4096], P(None, 'fsdp')
- fc_bias_grad: float32 [1, 4096], P(None, 'fsdp')
- out_weight_grad: float32 [1, 4096, 1024], P(None, 'fsdp')
- out_bias_grad: float32 [1, 1024], P(None, 'fsdp')
The draws below stay inside these ranges and needn't reach their ends.
Inputs may be any that keep to these rules, and one draw needn't show every extreme that they name: `block_order`: each row names every number from 0 to 15 once.
All inputs are finite; a program needn't handle non-finite values.
Results may differ from the reference program's by a relative error of at most 0.014.
Values may be sent and summed in bfloat16 or wider, within the bound.
A program may use at most 192 MiB of HBM per device.

```python
import math
from functools import partial
import jax
import jax.numpy as jnp
from jax import lax

D = 1024
HEADS = 16
HEAD_DIM = 64
FF = 4096
LAYERS = 1
BLK = 64
BLOCKS = 16
LEN = 1024
SEQS = 4


def levels(stream_key, shape, split, smallest, top_value):
    def one(axis_at, parts):
        draws = jax.random.uniform(jax.random.fold_in(jax.random.fold_in(stream_key, 6), axis_at), (parts,), jnp.float32, smallest / len(split), top_value / len(split))
        return jnp.repeat(jnp.exp(draws), shape[axis_at] // parts).reshape((-1,) + (1,) * (len(shape) - axis_at - 1))

    loudness = one(*split[0])
    for cut in split[1:]:
        loudness = loudness * one(*cut)
    return loudness


def centred(own_key, extent, deviation, bound, shards=(), held_as=jnp.bfloat16):
    level = levels(own_key, extent, shards, -0.22, 0.18) if shards else 1.0
    values = jax.random.normal(own_key, extent, jnp.float32) * deviation * level
    return jnp.minimum(jnp.maximum(values, -bound), bound).astype(held_as)


def setup_inputs(seed: int = 0) -> dict:
    keys = jax.random.split(jax.random.key(seed), 17)
    return {
        "tokens": centred(keys[0], (SEQS, LEN, D), 1.0, 6.0, ((0, 4), (1, 8))),
        "cotangent": centred(keys[1], (SEQS, LEN, D), 1.0, 6.0, ((0, 4), (1, 8)), jnp.float32),
        "block_order": jax.vmap(lambda own: jax.random.permutation(own, BLOCKS))(jax.random.split(keys[2], SEQS)).reshape((SEQS, BLOCKS)).astype(jnp.int32),
        "ln1_gain": jnp.clip(1.0 + 0.18 * jax.random.normal(keys[3], (LAYERS, D), jnp.float32), 0.099609375, 1.8984375).astype(jnp.bfloat16),
        "ln1_bias": centred(keys[4], (LAYERS, D), 0.3, 4.0, ((1, 4),)),
        "qkv_weight": centred(keys[5], (LAYERS, D, 3 * D), D ** -0.5, 0.1875, ((1, 4),)),
        "query_bias": centred(keys[6], (LAYERS, D), 0.5, 6.0, ((1, 4),)),
        "value_bias": centred(keys[7], (LAYERS, D), 0.5, 6.0, ((1, 4),)),
        "proj_weight": centred(keys[8], (LAYERS, D, D), (D // 16) ** -0.5, 0.75, ((1, 4),)),
        "proj_bias": centred(keys[9], (LAYERS, D), 0.3, 4.0, ((1, 4),)),
        "ln2_gain": jnp.clip(1.0 + 0.18 * jax.random.normal(keys[10], (LAYERS, D), jnp.float32), 0.099609375, 1.8984375).astype(jnp.bfloat16),
        "ln2_bias": centred(keys[11], (LAYERS, D), 0.3, 4.0, ((1, 4),)),
        "fc_weight": centred(keys[12], (LAYERS, D, FF), D ** -0.5, 0.1875, ((1, 4),)),
        "fc_bias": centred(keys[13], (LAYERS, FF), 0.5, 6.0, ((1, 4),)),
        "out_weight": centred(keys[14], (LAYERS, FF, D), FF ** -0.5, 0.09375, ((1, 4),)),
        "out_bias": centred(keys[15], (LAYERS, D), 0.3, 4.0, ((1, 4),)),
    }


NORM_EPS = 1e-05
GELU_SCALE = math.sqrt(2.0 / math.pi)

def layer_norm(values_in, gain_vec, shift_vec):
    center = values_in - lax.optimization_barrier(jnp.mean(values_in, axis=-1, keepdims=True))
    variance = lax.optimization_barrier(jnp.mean(center * center, axis=-1, keepdims=True))
    inverse = lax.rsqrt(variance + NORM_EPS)
    normed = center * inverse
    return (normed * gain_vec + shift_vec, normed, inverse)

def norm_back(upstream, normed, inverse, gain_vec):
    scaled = upstream * gain_vec
    inner_term = scaled - lax.optimization_barrier(jnp.mean(scaled, axis=-1, keepdims=True)) - normed * lax.optimization_barrier(jnp.mean(scaled * normed, axis=-1, keepdims=True))
    return (inverse * inner_term, lax.optimization_barrier(jnp.sum(upstream * normed, axis=0)), lax.optimization_barrier(jnp.sum(upstream, axis=0)))

def gelu_pair(pre_act):
    inner_arg = GELU_SCALE * (pre_act + 0.044715 * pre_act * pre_act * pre_act)
    tangent = jnp.tanh(inner_arg)
    output = 0.5 * pre_act * (1.0 + tangent)
    gelu_slope = 0.5 * (1.0 + tangent) + 0.5 * pre_act * (1.0 - tangent * tangent) * GELU_SCALE * (1.0 + 3.0 * 0.044715 * pre_act * pre_act)
    return (output, gelu_slope)

def attend_rows(queries, key_rows, value_rows, positions):
    total_rows = queries.shape[0]
    block_width = math.gcd(total_rows, 512)
    block_count = total_rows // block_width
    query_blocks = queries.reshape(block_count, block_width, HEADS, HEAD_DIM)
    pos_blocks = positions.reshape(block_count, block_width)
    key_heads = key_rows.reshape(total_rows, HEADS, HEAD_DIM).astype(jnp.float32)
    value_heads = value_rows.reshape(total_rows, HEADS, HEAD_DIM).astype(jnp.float32)

    def one_block(inputs):
        query_blk, pos_blk = inputs
        scores = jnp.einsum('qhd,khd->hqk', query_blk.astype(jnp.float32), key_heads) * 0.125
        allowed = positions[None, None, :] <= pos_blk[None, :, None]
        top_score = lax.optimization_barrier(jnp.max(jnp.where(allowed, scores, -1e+30), axis=2))
        attn_probs = jnp.where(allowed, jnp.exp(scores - top_score[:, :, None]), 0.0)
        weight_sum = lax.optimization_barrier(jnp.sum(attn_probs, axis=2))
        mixed_out = jnp.einsum('hqk,khd->qhd', attn_probs.astype(jnp.bfloat16).astype(jnp.float32), value_heads)
        mixed_out = mixed_out / weight_sum.T[:, :, None]
        return (mixed_out.reshape(block_width, D).astype(jnp.bfloat16), top_score + jnp.log(weight_sum))
    block_outs, block_lse = lax.map(one_block, (query_blocks, pos_blocks))
    return (block_outs.reshape(total_rows, D), jnp.transpose(block_lse, (1, 0, 2)).reshape(HEADS, total_rows))

def attend_back(queries, key_rows, value_rows, att_out, grad_att, lse_rows, positions):
    total_rows = queries.shape[0]
    block_width = math.gcd(total_rows, 512)
    block_count = total_rows // block_width
    query_heads = queries.reshape(total_rows, HEADS, HEAD_DIM).astype(jnp.float32)
    key_heads = key_rows.reshape(total_rows, HEADS, HEAD_DIM).astype(jnp.float32)
    value_heads = value_rows.reshape(total_rows, HEADS, HEAD_DIM).astype(jnp.float32)
    grad_heads = grad_att.reshape(total_rows, HEADS, HEAD_DIM).astype(jnp.float32)
    delta_rows = lax.optimization_barrier(jnp.sum(grad_heads * att_out.reshape(total_rows, HEADS, HEAD_DIM).astype(jnp.float32), axis=2))
    inputs_all = (query_heads.reshape(block_count, block_width, HEADS, HEAD_DIM), grad_heads.reshape(block_count, block_width, HEADS, HEAD_DIM), jnp.transpose(lse_rows.reshape(HEADS, block_count, block_width), (1, 0, 2)), delta_rows.reshape(block_count, block_width, HEADS), positions.reshape(block_count, block_width))

    def one_block(carry_state, inputs):
        grad_keys, grad_values = carry_state
        query_blk, grad_blk, lse_blk, delta_blk, pos_blk = inputs
        scores = jnp.einsum('qhd,khd->hqk', query_blk, key_heads) * 0.125
        allowed = positions[None, None, :] <= pos_blk[None, :, None]
        attn_probs = jnp.where(allowed, jnp.exp(scores - lse_blk[:, :, None]), 0.0)
        grad_values = grad_values + jnp.einsum('hqk,qhd->khd', attn_probs.astype(jnp.bfloat16).astype(jnp.float32), grad_blk)
        grad_probs = jnp.einsum('qhd,khd->hqk', grad_blk, value_heads)
        grad_scores = (attn_probs * (grad_probs - delta_blk.T[:, :, None]) * 0.125).astype(jnp.bfloat16).astype(jnp.float32)
        grad_query = jnp.einsum('hqk,khd->qhd', grad_scores, key_heads)
        grad_keys = grad_keys + jnp.einsum('hqk,qhd->khd', grad_scores, query_blk)
        return ((grad_keys, grad_values), grad_query.reshape(block_width, D))
    zero_state = jnp.zeros((total_rows, HEADS, HEAD_DIM), jnp.float32)
    (grad_keys, grad_values), grad_queries = lax.scan(one_block, (zero_state, zero_state), inputs_all)
    return (grad_queries.reshape(total_rows, D), grad_keys.reshape(total_rows, D), grad_values.reshape(total_rows, D))

def layer_forward(stream, weights_now, attend_fn):
    gain_one, shift_one, qkv_w, query_b, value_b, proj_w, proj_b, gain_two, shift_two, fc_w, fc_b, out_w, out_b = weights_now
    normed_out, normed_one, inverse_one = layer_norm(stream, gain_one.astype(jnp.float32), shift_one.astype(jnp.float32))
    attn_in = normed_out.astype(jnp.bfloat16)
    projected = jnp.dot(attn_in, qkv_w, preferred_element_type=jnp.float32)
    queries = (projected[:, :D] + query_b.astype(jnp.float32)).astype(jnp.bfloat16)
    key_rows = projected[:, D:2 * D].astype(jnp.bfloat16)
    value_rows = (projected[:, 2 * D:] + value_b.astype(jnp.float32)).astype(jnp.bfloat16)
    att_out, lse_rows = attend_fn(queries, key_rows, value_rows)
    middle = stream + jnp.dot(att_out, proj_w, preferred_element_type=jnp.float32) + proj_b.astype(jnp.float32)
    normed_mid, normed_two, inverse_two = layer_norm(middle, gain_two.astype(jnp.float32), shift_two.astype(jnp.float32))
    mlp_in = normed_mid.astype(jnp.bfloat16)
    pre_act = jnp.dot(mlp_in, fc_w, preferred_element_type=jnp.float32) + fc_b.astype(jnp.float32)
    activated, gelu_slope = gelu_pair(pre_act)
    act_rows = activated.astype(jnp.bfloat16)
    result = middle + jnp.dot(act_rows, out_w, preferred_element_type=jnp.float32) + out_b.astype(jnp.float32)
    record = (normed_one, inverse_one, attn_in, queries, key_rows, value_rows, att_out, lse_rows, normed_two, inverse_two, mlp_in, gelu_slope, act_rows)
    return (result, record)

def layer_backward(upstream, weights_now, record, back_fn):
    gain_one, shift_one, qkv_w, query_b, value_b, proj_w, proj_b, gain_two, shift_two, fc_w, fc_b, out_w, out_b = weights_now
    normed_one, inverse_one, attn_in, queries, key_rows, value_rows, att_out, lse_rows, normed_two, inverse_two, mlp_in, gelu_slope, act_rows = record
    up_rows = upstream.astype(jnp.bfloat16)
    grad_out_w = jnp.dot(act_rows.T, up_rows, preferred_element_type=jnp.float32)
    grad_out_b = lax.optimization_barrier(jnp.sum(upstream, axis=0))
    grad_act = jnp.dot(up_rows, out_w.T, preferred_element_type=jnp.float32)
    grad_pre = grad_act * gelu_slope
    grad_pre_rows = grad_pre.astype(jnp.bfloat16)
    grad_fc_w = jnp.dot(mlp_in.T, grad_pre_rows, preferred_element_type=jnp.float32)
    grad_fc_b = lax.optimization_barrier(jnp.sum(grad_pre, axis=0))
    grad_mlp_in = jnp.dot(grad_pre_rows, fc_w.T, preferred_element_type=jnp.float32)
    back_two, grad_gain_two, grad_shift_two = norm_back(grad_mlp_in, normed_two, inverse_two, gain_two.astype(jnp.float32))
    mid_grad = upstream + back_two
    mid_rows = mid_grad.astype(jnp.bfloat16)
    grad_proj_w = jnp.dot(att_out.T, mid_rows, preferred_element_type=jnp.float32)
    grad_proj_b = lax.optimization_barrier(jnp.sum(mid_grad, axis=0))
    grad_att = jnp.dot(mid_rows, proj_w.T, preferred_element_type=jnp.float32).astype(jnp.bfloat16)
    grad_query, grad_key, grad_value = back_fn(queries, key_rows, value_rows, att_out, grad_att, lse_rows)
    grad_query_b = lax.optimization_barrier(jnp.sum(grad_query, axis=0))
    grad_value_b = lax.optimization_barrier(jnp.sum(grad_value, axis=0))
    grad_qkv_rows = jnp.concatenate([grad_query, grad_key, grad_value], axis=1).astype(jnp.bfloat16)
    grad_qkv_w = jnp.dot(attn_in.T, grad_qkv_rows, preferred_element_type=jnp.float32)
    grad_attn_in = jnp.dot(grad_qkv_rows, qkv_w.T, preferred_element_type=jnp.float32)
    back_one, grad_gain_one, grad_shift_one = norm_back(grad_attn_in, normed_one, inverse_one, gain_one.astype(jnp.float32))
    new_upstream = mid_grad + back_one
    grads_now = (grad_gain_one, grad_shift_one, grad_qkv_w, grad_query_b, grad_value_b, grad_proj_w, grad_proj_b, grad_gain_two, grad_shift_two, grad_fc_w, grad_fc_b, grad_out_w, grad_out_b)
    return (new_upstream, grads_now)

def reference(tokens, cotangent, block_order, ln1_gain, ln1_bias, qkv_weight, query_bias, value_bias, proj_weight, proj_bias, ln2_gain, ln2_bias, fc_weight, fc_bias, out_weight, out_bias):
    params = (ln1_gain, ln1_bias, qkv_weight, query_bias, value_bias, proj_weight, proj_bias, ln2_gain, ln2_bias, fc_weight, fc_bias, out_weight, out_bias)
    zero_grads = tuple((jnp.zeros(param_stack.shape, jnp.float32) for param_stack in params))

    def one_sequence(totals, inputs):
        seq_tokens, seq_cot, order_row = inputs
        index_all = jnp.arange(LEN, dtype=jnp.int32)
        positions = (order_row[index_all // BLK] * BLK + index_all % BLK).astype(jnp.int32)
        stream = seq_tokens.astype(jnp.float32)
        saved_records = []
        for layer_idx in range(LAYERS):
            weights_now = tuple((param_stack[layer_idx] for param_stack in params))
            stream, record = layer_forward(stream, weights_now, partial(attend_rows, positions=positions))
            saved_records.append(record)
        upstream = seq_cot.astype(jnp.float32)
        layer_grads = [None] * LAYERS
        for layer_idx in reversed(range(LAYERS)):
            weights_now = tuple((param_stack[layer_idx] for param_stack in params))
            upstream, layer_grads[layer_idx] = layer_backward(upstream, weights_now, saved_records[layer_idx], partial(attend_back, positions=positions))
        new_totals = tuple((totals[param_idx] + jnp.stack([layer_grads[layer_idx][param_idx] for layer_idx in range(LAYERS)]) for param_idx in range(len(params))))
        return (new_totals, (stream, upstream))
    totals, (outputs, input_grads) = lax.scan(one_sequence, zero_grads, (tokens, cotangent, block_order))
    return (outputs, input_grads, totals[0], totals[1], totals[2], totals[3], totals[4], totals[5], totals[6], totals[7], totals[8], totals[9], totals[10], totals[11], totals[12])
```

```python
import math

import jax
import jax.numpy as jnp
from jax import lax
from jax.experimental import pallas as pl
from jax.experimental.pallas import tpu as pltpu
from jax.sharding import Mesh
from jax.sharding import PartitionSpec as P

D = 1024
HEADS = 16
HEAD_DIM = 64
LAYERS = 1
CTX = ("chip", "core")


NORM_EPS = 1e-05
GELU_SCALE = math.sqrt(2.0 / math.pi)


def layer_norm(values_in, gain_vec, shift_vec):
    center = values_in - jnp.mean(values_in, axis=-1, keepdims=True)
    variance = jnp.mean(center * center, axis=-1, keepdims=True)
    inverse = lax.rsqrt(variance + NORM_EPS)
    normed = center * inverse
    return (normed * gain_vec + shift_vec, normed, inverse)


def norm_back(upstream, normed, inverse, gain_vec):
    scaled = upstream * gain_vec
    inner_term = (
        scaled
        - jnp.mean(scaled, axis=-1, keepdims=True)
        - normed * jnp.mean(scaled * normed, axis=-1, keepdims=True)
    )
    return (inverse * inner_term, jnp.sum(upstream * normed, axis=0), jnp.sum(upstream, axis=0))


def gelu_pair(pre_act):
    inner_arg = GELU_SCALE * (pre_act + 0.044715 * pre_act * pre_act * pre_act)
    tangent = jnp.tanh(inner_arg)
    output = 0.5 * pre_act * (1.0 + tangent)
    gelu_slope = 0.5 * (1.0 + tangent) + 0.5 * pre_act * (1.0 - tangent * tangent) * GELU_SCALE * (
        1.0 + 3.0 * 0.044715 * pre_act * pre_act
    )
    return (output, gelu_slope)


def token_positions(order_row, row_total, half_block):
    slots = order_row.shape[0]
    return (order_row[:, None] * half_block + jnp.arange(half_block, dtype=jnp.int32)).reshape(
        slots * half_block
    )


def dot_nt(left, right):
    return lax.dot_general(left, right, (((1,), (1,)), ((), ())), preferred_element_type=jnp.float32)


def dot_tn(left, right):
    return lax.dot_general(left, right, (((0,), (0,)), ((), ())), preferred_element_type=jnp.float32)


def attend_kernel(q_ref, k_ref, v_ref, qpos_ref, kpos_ref, out_ref, lse_ref):
    allowed = kpos_ref[...] <= qpos_ref[...]
    heads = q_ref.shape[1] // HEAD_DIM
    outs, lses = [], []
    for h in range(heads):
        cols = slice(h * HEAD_DIM, (h + 1) * HEAD_DIM)
        scores = dot_nt(q_ref[:, cols], k_ref[:, cols]) * 0.125
        scores = jnp.where(allowed, scores, -1e30)
        top = jnp.max(scores, axis=1, keepdims=True)
        probs = jnp.exp(scores - top)
        total = jnp.sum(probs, axis=1, keepdims=True)
        acc = jnp.dot(probs.astype(jnp.bfloat16), v_ref[:, cols], preferred_element_type=jnp.float32)
        outs.append((acc / total).astype(jnp.bfloat16))
        lses.append(top + jnp.log(total))
    out_ref[...] = jnp.concatenate(outs, axis=1) if heads > 1 else outs[0]
    lse_ref[...] = jnp.concatenate(lses, axis=1) if heads > 1 else lses[0]


def attend_back_kernel(
    q_ref, k_ref, v_ref, qpos_ref, kpos_ref, out_ref, grad_ref, lse_ref, dq_ref, dk_ref, dv_ref
):
    step = pl.program_id(0)
    allowed = kpos_ref[...] <= qpos_ref[...]
    heads = q_ref.shape[1] // HEAD_DIM
    dqs, dks, dvs = [], [], []
    for h in range(heads):
        cols = slice(h * HEAD_DIM, (h + 1) * HEAD_DIM)
        queries, keys, values, grads = q_ref[:, cols], k_ref[:, cols], v_ref[:, cols], grad_ref[:, cols]
        delta = jnp.sum(
            grads.astype(jnp.float32) * out_ref[:, cols].astype(jnp.float32), axis=1, keepdims=True
        )
        scores = dot_nt(queries, keys) * 0.125
        probs = jnp.exp(jnp.where(allowed, scores - lse_ref[:, h : h + 1], -1e30))
        grad_scores = (probs * (dot_nt(grads, values) - delta) * 0.125).astype(jnp.bfloat16)
        dvs.append(dot_tn(probs.astype(jnp.bfloat16), grads))
        dqs.append(jnp.dot(grad_scores, keys, preferred_element_type=jnp.float32))
        dks.append(dot_tn(grad_scores, queries))
    join = lambda parts: jnp.concatenate(parts, axis=1) if heads > 1 else parts[0]
    dq_ref[...] = join(dqs)

    @pl.when(step == 0)
    def _():
        dk_ref[...] = join(dks)
        dv_ref[...] = join(dvs)

    @pl.when(step > 0)
    def _():
        dk_ref[...] += join(dks)
        dv_ref[...] += join(dvs)


def attention_specs(total, width, heads, tile):
    row = pl.BlockSpec((tile, width), lambda i: (i, 0))
    full = pl.BlockSpec((total, width), lambda i: (0, 0))
    qpos = pl.BlockSpec((tile, 1), lambda i: (i, 0))
    kpos = pl.BlockSpec((1, total), lambda i: (0, 0))
    lse = pl.BlockSpec((tile, heads), lambda i: (i, 0))
    return row, full, qpos, kpos, lse


def run_attend(queries, keys, values, position):
    total, width = queries.shape
    heads = width // HEAD_DIM
    tile = 256
    row, full, qpos, kpos, lse = attention_specs(total, width, heads, tile)
    return pl.pallas_call(
        attend_kernel,
        grid=(total // tile,),
        in_specs=[row, full, full, qpos, kpos],
        out_specs=[row, lse],
        out_shape=[
            jax.ShapeDtypeStruct((total, width), jnp.bfloat16),
            jax.ShapeDtypeStruct((total, heads), jnp.float32),
        ],
        compiler_params=pltpu.CompilerParams(vmem_limit_bytes=40 * 1024 * 1024),
        cost_estimate=pl.CostEstimate(
            flops=4 * total * total * width, bytes_accessed=8 * total * width, transcendentals=total * total * heads
        ),
    )(queries, keys, values, position[:, None], position[None, :])


def run_attend_back(queries, keys, values, position, att_out, grad_att, lse_rows):
    total, width = queries.shape
    heads = width // HEAD_DIM
    tile = 256
    row, full, qpos, kpos, lse = attention_specs(total, width, heads, tile)
    shape = jax.ShapeDtypeStruct((total, width), jnp.float32)
    return pl.pallas_call(
        attend_back_kernel,
        grid=(total // tile,),
        in_specs=[row, full, full, qpos, kpos, row, row, lse],
        out_specs=[row, full, full],
        out_shape=[shape, shape, shape],
        compiler_params=pltpu.CompilerParams(vmem_limit_bytes=40 * 1024 * 1024),
        cost_estimate=pl.CostEstimate(
            flops=10 * total * total * width, bytes_accessed=22 * total * width, transcendentals=total * total * heads
        ),
    )(queries, keys, values, position[:, None], position[None, :], att_out, grad_att, lse_rows)


def swap_cores(rows):
    return lax.ppermute(rows, "core", [(0, 1), (1, 0)])


def to_heads(rows, parts):
    count = rows.shape[0]
    n = lax.axis_size(CTX)
    width = D // n
    stacked = rows.reshape(count, parts, n, width).transpose(2, 0, 1, 3).reshape(n, count, parts * width)
    moved = lax.all_to_all(stacked, CTX, split_axis=0, concat_axis=0, tiled=True)
    moved = moved.reshape(n * count, parts * width)
    return tuple(moved[:, p * width : (p + 1) * width] for p in range(parts))


def to_tokens(columns):
    parts = len(columns)
    n = lax.axis_size(CTX)
    total, width = columns[0].shape
    count = total // n
    joined = jnp.concatenate(columns, axis=1).reshape(n, count, parts * width)
    moved = lax.all_to_all(joined, CTX, split_axis=0, concat_axis=0, tiled=True)
    return moved.reshape(n, count, parts, width).transpose(1, 2, 0, 3).reshape(count, parts * n * width)


def layer_forward(stream, weights_now, position):
    (
        gain_one,
        shift_one,
        qkv_w,
        query_b,
        value_b,
        proj_w,
        proj_b,
        gain_two,
        shift_two,
        fc_w,
        fc_b,
        out_w,
        out_b,
    ) = weights_now
    normed_out, normed_one, inverse_one = layer_norm(
        stream, gain_one.astype(jnp.float32), shift_one.astype(jnp.float32)
    )
    attn_in = normed_out.astype(jnp.bfloat16)
    projected = jnp.dot(attn_in, qkv_w, preferred_element_type=jnp.float32)
    bias_row = jnp.concatenate([query_b, jnp.zeros_like(query_b), value_b]).astype(jnp.float32)
    qkv_rows = (projected + bias_row).astype(jnp.bfloat16)
    queries, key_rows, value_rows = to_heads(qkv_rows, 3)
    att_heads, lse_rows = run_attend(queries, key_rows, value_rows, position)
    att_out = to_tokens((att_heads,))
    middle = (
        stream
        + jnp.dot(att_out, proj_w, preferred_element_type=jnp.float32)
        + proj_b.astype(jnp.float32)
    )
    normed_mid, normed_two, inverse_two = layer_norm(
        middle, gain_two.astype(jnp.float32), shift_two.astype(jnp.float32)
    )
    mlp_in = normed_mid.astype(jnp.bfloat16)
    pre_act = jnp.dot(mlp_in, fc_w, preferred_element_type=jnp.float32) + fc_b.astype(jnp.float32)
    activated, gelu_slope = gelu_pair(pre_act)
    act_rows = activated.astype(jnp.bfloat16)
    result = (
        middle
        + jnp.dot(act_rows, out_w, preferred_element_type=jnp.float32)
        + out_b.astype(jnp.float32)
    )
    record = (
        normed_one,
        inverse_one,
        attn_in,
        queries,
        key_rows,
        value_rows,
        att_heads,
        att_out,
        lse_rows,
        normed_two,
        inverse_two,
        mlp_in,
        gelu_slope,
        act_rows,
    )
    return (result, record)


def layer_backward(upstream, weights_now, record, position):
    (
        gain_one,
        shift_one,
        qkv_w,
        query_b,
        value_b,
        proj_w,
        proj_b,
        gain_two,
        shift_two,
        fc_w,
        fc_b,
        out_w,
        out_b,
    ) = weights_now
    (
        normed_one,
        inverse_one,
        attn_in,
        queries,
        key_rows,
        value_rows,
        att_heads,
        att_out,
        lse_rows,
        normed_two,
        inverse_two,
        mlp_in,
        gelu_slope,
        act_rows,
    ) = record
    up_rows = upstream.astype(jnp.bfloat16)
    grad_out_b = jnp.sum(upstream, axis=0)
    grad_act = jnp.dot(up_rows, out_w.T, preferred_element_type=jnp.float32)
    grad_pre = grad_act * gelu_slope
    grad_pre_rows = grad_pre.astype(jnp.bfloat16)
    grad_fc_b = jnp.sum(grad_pre, axis=0)
    grad_mlp_in = jnp.dot(grad_pre_rows, fc_w.T, preferred_element_type=jnp.float32)
    back_two, grad_gain_two, grad_shift_two = norm_back(
        grad_mlp_in, normed_two, inverse_two, gain_two.astype(jnp.float32)
    )
    mid_grad = upstream + back_two
    mid_rows = mid_grad.astype(jnp.bfloat16)
    grad_proj_b = jnp.sum(mid_grad, axis=0)
    grad_att = jnp.dot(mid_rows, proj_w.T, preferred_element_type=jnp.float32).astype(jnp.bfloat16)
    (grad_heads,) = to_heads(grad_att, 1)
    grad_query, grad_key, grad_value = run_attend_back(
        queries, key_rows, value_rows, position, att_heads, grad_heads, lse_rows
    )
    head_sums = jnp.stack([jnp.sum(grad_query, axis=0), jnp.sum(grad_value, axis=0)])
    mine = lax.axis_index(CTX) * head_sums.shape[1]
    spread = lax.dynamic_update_slice(jnp.zeros((2, D), jnp.float32), head_sums, (0, mine))
    grad_query_b, grad_value_b = spread[0], spread[1]
    grad_qkv_rows = to_tokens(
        tuple(part.astype(jnp.bfloat16) for part in (grad_query, grad_key, grad_value))
    )
    grad_attn_in = jnp.dot(grad_qkv_rows, qkv_w.T, preferred_element_type=jnp.float32)
    back_one, grad_gain_one, grad_shift_one = norm_back(
        grad_attn_in, normed_one, inverse_one, gain_one.astype(jnp.float32)
    )
    new_upstream = mid_grad + back_one
    vectors = (
        grad_gain_one,
        grad_shift_one,
        grad_query_b,
        grad_value_b,
        grad_proj_b,
        grad_gain_two,
        grad_shift_two,
        grad_fc_b,
        grad_out_b,
    )
    row_pairs = (
        (attn_in, grad_qkv_rows),
        (att_out, mid_rows),
        (mlp_in, grad_pre_rows),
        (act_rows, up_rows),
    )
    return (new_upstream, vectors, row_pairs)


def assemble(vectors, matrices):
    return (
        vectors[0],
        vectors[1],
        matrices[0],
        vectors[2],
        vectors[3],
        matrices[1],
        vectors[4],
        vectors[5],
        vectors[6],
        matrices[2],
        vectors[7],
        matrices[3],
        vectors[8],
    )


def shards(
    tokens,
    cotangent,
    block_order,
    ln1_gain,
    ln1_bias,
    qkv_weight,
    query_bias,
    value_bias,
    proj_weight,
    proj_bias,
    ln2_gain,
    ln2_bias,
    fc_weight,
    fc_bias,
    out_weight,
    out_bias,
):
    row_count = tokens.shape[1]
    contexts = lax.axis_size(CTX)
    groups = lax.axis_size("fsdp")
    slots = block_order.shape[1]
    half_block = row_count * contexts // slots
    position = token_positions(block_order[0], row_count * contexts, half_block)
    stream = tokens[0].astype(jnp.float32)
    vectors_in = (
        ln1_gain, ln1_bias, query_bias, value_bias, proj_bias, ln2_gain, ln2_bias, fc_bias, out_bias,
    )
    sizes = [v.shape[1] for v in vectors_in]
    gathered = lax.all_gather(jnp.concatenate([v[0] for v in vectors_in]), "fsdp", axis=0)
    gathered_vectors = []
    start = 0
    for size in sizes:
        gathered_vectors.append(gathered[:, start : start + size].reshape(groups * size))
        start += size
    me = lax.axis_index(CTX)

    def gather_weight(weight):
        rows = weight.shape[1] // contexts
        piece = lax.dynamic_slice_in_dim(weight[0], me * rows, rows, axis=0)
        return lax.all_gather(piece, ("fsdp",) + CTX, axis=0, tiled=True)

    qkv_full = gather_weight(qkv_weight)
    proj_full = gather_weight(proj_weight)
    fc_full = gather_weight(fc_weight)
    out_full = gather_weight(out_weight)
    g = gathered_vectors
    full_weights = (
        g[0], g[1], qkv_full, g[2], g[3], proj_full, g[4], g[5], g[6], fc_full, g[7], out_full, g[8],
    )
    stream, record = layer_forward(stream, full_weights, position)
    upstream, vectors, row_pairs = layer_backward(cotangent[0], full_weights, record, position)
    matrices = []
    for left, right in row_pairs:
        features = left.shape[1] // (groups * 2)
        pieces = left.reshape(row_count, groups, 2, features)
        pieces = pieces.transpose(2, 0, 1, 3).reshape(2, row_count, groups * features)
        core = lax.axis_index("core")
        own_half = lax.dynamic_index_in_dim(pieces, core, 0, keepdims=False)
        sent_half = lax.dynamic_index_in_dim(pieces, 1 - core, 0, keepdims=False)
        left_half = jnp.concatenate([own_half, swap_cores(sent_half)])
        right_pair = jnp.concatenate([right, swap_cores(right)])
        terms = dot_tn(left_half, right_pair).astype(jnp.bfloat16)
        part = lax.psum_scatter(terms, ("fsdp", "chip"), scatter_dimension=0, tiled=True)
        total = lax.all_gather(part, ("core", "chip"), axis=0, tiled=True)
        matrices.append(total.astype(jnp.float32)[None])
    packed = jnp.concatenate([v.reshape(groups, -1) for v in vectors], axis=1)
    summed = lax.psum(packed, ("fsdp",) + CTX)
    own = lax.dynamic_index_in_dim(summed, lax.axis_index("fsdp"), 0, keepdims=True)
    vector_parts = []
    start = 0
    for v in vectors:
        size = v.shape[0] // groups
        vector_parts.append(own[:, start : start + size])
        start += size
    return (stream[None], upstream[None]) + assemble(vector_parts, matrices)


def solution(mesh):
    contexts, groups = mesh.devices.shape
    split_mesh = Mesh(mesh.devices.reshape(contexts // 2, 2, groups), ("chip", "core", "fsdp"))
    placed = (
        P("fsdp", CTX, None),
        P("fsdp", CTX, None),
        P("fsdp", None),
        P(None, "fsdp"),
        P(None, "fsdp"),
        P(None, "fsdp", None),
        P(None, "fsdp"),
        P(None, "fsdp"),
        P(None, "fsdp", None),
        P(None, "fsdp"),
        P(None, "fsdp"),
        P(None, "fsdp"),
        P(None, "fsdp", None),
        P(None, "fsdp"),
        P(None, "fsdp", None),
        P(None, "fsdp"),
    )
    return jax.shard_map(
        shards,
        mesh=split_mesh,
        in_specs=placed,
        out_specs=(
            P("fsdp", CTX, None),
            P("fsdp", CTX, None),
            P(None, "fsdp"),
            P(None, "fsdp"),
            P(None, "fsdp", None),
            P(None, "fsdp"),
            P(None, "fsdp"),
            P(None, "fsdp", None),
            P(None, "fsdp"),
            P(None, "fsdp"),
            P(None, "fsdp"),
            P(None, "fsdp", None),
            P(None, "fsdp"),
            P(None, "fsdp", None),
            P(None, "fsdp"),
        ),
        check_vma=False,
    )
```

```python
import math

import jax
import jax.numpy as jnp
from jax import lax
from jax.experimental import pallas as pl
from jax.experimental.pallas import tpu as pltpu
from jax.sharding import Mesh
from jax.sharding import PartitionSpec as P

D = 1024
HEADS = 16
HEAD_DIM = 64
LAYERS = 1
CTX = ("chip", "core")


NORM_EPS = 1e-05
GELU_SCALE = math.sqrt(2.0 / math.pi)


def layer_norm(values_in, gain_vec, shift_vec):
    center = values_in - jnp.mean(values_in, axis=-1, keepdims=True)
    variance = jnp.mean(center * center, axis=-1, keepdims=True)
    inverse = lax.rsqrt(variance + NORM_EPS)
    normed = center * inverse
    return (normed * gain_vec + shift_vec, normed, inverse)


def norm_back(upstream, normed, inverse, gain_vec):
    scaled = upstream * gain_vec
    inner_term = (
        scaled
        - jnp.mean(scaled, axis=-1, keepdims=True)
        - normed * jnp.mean(scaled * normed, axis=-1, keepdims=True)
    )
    return (inverse * inner_term, jnp.sum(upstream * normed, axis=0), jnp.sum(upstream, axis=0))


def gelu_pair(pre_act):
    inner_arg = GELU_SCALE * (pre_act + 0.044715 * pre_act * pre_act * pre_act)
    tangent = jnp.tanh(inner_arg)
    output = 0.5 * pre_act * (1.0 + tangent)
    gelu_slope = 0.5 * (1.0 + tangent) + 0.5 * pre_act * (1.0 - tangent * tangent) * GELU_SCALE * (
        1.0 + 3.0 * 0.044715 * pre_act * pre_act
    )
    return (output, gelu_slope)


def token_positions(order_row, row_total, half_block):
    slots = order_row.shape[0]
    return (order_row[:, None] * half_block + jnp.arange(half_block, dtype=jnp.int32)).reshape(
        slots * half_block
    )


def dot_nt(left, right):
    return lax.dot_general(left, right, (((1,), (1,)), ((), ())), preferred_element_type=jnp.float32)


def dot_tn(left, right):
    return lax.dot_general(left, right, (((0,), (0,)), ((), ())), preferred_element_type=jnp.float32)


def attend_kernel(q_ref, k_ref, v_ref, qpos_ref, kpos_ref, out_ref, lse_ref):
    allowed = kpos_ref[...] <= qpos_ref[...]
    heads = q_ref.shape[1] // HEAD_DIM
    outs, lses = [], []
    for h in range(heads):
        cols = slice(h * HEAD_DIM, (h + 1) * HEAD_DIM)
        scores = dot_nt(q_ref[:, cols], k_ref[:, cols]) * 0.125
        scores = jnp.where(allowed, scores, -1e30)
        top = jnp.max(scores, axis=1, keepdims=True)
        probs = jnp.exp(scores - top)
        total = jnp.sum(probs, axis=1, keepdims=True)
        acc = jnp.dot(probs.astype(jnp.bfloat16), v_ref[:, cols], preferred_element_type=jnp.float32)
        outs.append((acc / total).astype(jnp.bfloat16))
        lses.append(top + jnp.log(total))
    out_ref[...] = jnp.concatenate(outs, axis=1) if heads > 1 else outs[0]
    lse_ref[...] = jnp.concatenate(lses, axis=1) if heads > 1 else lses[0]


def attend_back_kernel(
    q_ref, k_ref, v_ref, qpos_ref, kpos_ref, out_ref, grad_ref, lse_ref, dq_ref, dk_ref, dv_ref
):
    step = pl.program_id(0)
    allowed = kpos_ref[...] <= qpos_ref[...]
    heads = q_ref.shape[1] // HEAD_DIM
    dqs, dks, dvs = [], [], []
    for h in range(heads):
        cols = slice(h * HEAD_DIM, (h + 1) * HEAD_DIM)
        queries, keys, values, grads = q_ref[:, cols], k_ref[:, cols], v_ref[:, cols], grad_ref[:, cols]
        delta = jnp.sum(
            grads.astype(jnp.float32) * out_ref[:, cols].astype(jnp.float32), axis=1, keepdims=True
        )
        scores = dot_nt(queries, keys) * 0.125
        probs = jnp.exp(jnp.where(allowed, scores - lse_ref[:, h : h + 1], -1e30))
        grad_scores = (probs * (dot_nt(grads, values) - delta) * 0.125).astype(jnp.bfloat16)
        dvs.append(dot_tn(probs.astype(jnp.bfloat16), grads))
        dqs.append(jnp.dot(grad_scores, keys, preferred_element_type=jnp.float32))
        dks.append(dot_tn(grad_scores, queries))
    join = lambda parts: jnp.concatenate(parts, axis=1) if heads > 1 else parts[0]
    dq_ref[...] = join(dqs)

    @pl.when(step == 0)
    def _():
        dk_ref[...] = join(dks)
        dv_ref[...] = join(dvs)

    @pl.when(step > 0)
    def _():
        dk_ref[...] += join(dks)
        dv_ref[...] += join(dvs)


def attention_specs(total, width, heads, tile):
    row = pl.BlockSpec((tile, width), lambda i: (i, 0))
    full = pl.BlockSpec((total, width), lambda i: (0, 0))
    qpos = pl.BlockSpec((tile, 1), lambda i: (i, 0))
    kpos = pl.BlockSpec((1, total), lambda i: (0, 0))
    lse = pl.BlockSpec((tile, heads), lambda i: (i, 0))
    return row, full, qpos, kpos, lse


def run_attend(queries, keys, values, position):
    total, width = queries.shape
    heads = width // HEAD_DIM
    tile = 256
    row, full, qpos, kpos, lse = attention_specs(total, width, heads, tile)
    return pl.pallas_call(
        attend_kernel,
        grid=(total // tile,),
        in_specs=[row, full, full, qpos, kpos],
        out_specs=[row, lse],
        out_shape=[
            jax.ShapeDtypeStruct((total, width), jnp.bfloat16),
            jax.ShapeDtypeStruct((total, heads), jnp.float32),
        ],
        compiler_params=pltpu.CompilerParams(vmem_limit_bytes=40 * 1024 * 1024),
        cost_estimate=pl.CostEstimate(
            flops=4 * total * total * width, bytes_accessed=8 * total * width, transcendentals=total * total * heads
        ),
    )(queries, keys, values, position[:, None], position[None, :])


def run_attend_back(queries, keys, values, position, att_out, grad_att, lse_rows):
    total, width = queries.shape
    heads = width // HEAD_DIM
    tile = 256
    row, full, qpos, kpos, lse = attention_specs(total, width, heads, tile)
    shape = jax.ShapeDtypeStruct((total, width), jnp.float32)
    return pl.pallas_call(
        attend_back_kernel,
        grid=(total // tile,),
        in_specs=[row, full, full, qpos, kpos, row, row, lse],
        out_specs=[row, full, full],
        out_shape=[shape, shape, shape],
        compiler_params=pltpu.CompilerParams(vmem_limit_bytes=40 * 1024 * 1024),
        cost_estimate=pl.CostEstimate(
            flops=10 * total * total * width, bytes_accessed=22 * total * width, transcendentals=total * total * heads
        ),
    )(queries, keys, values, position[:, None], position[None, :], att_out, grad_att, lse_rows)


def swap_cores(rows):
    return lax.ppermute(rows, "core", [(0, 1), (1, 0)])


def swap_bit(rows, axis, bit):
    count = lax.axis_size(axis)
    return lax.ppermute(rows, axis, [(i, i ^ (1 << bit)) for i in range(count)])


def bits_of(axis):
    return lax.axis_size(axis).bit_length() - 1


def bit_order(reverse):
    order = list(range(bits_of("chip")))
    return order[::-1] if reverse else order


def halve(block, axis, order):
    count = bits_of(axis)
    block = block.reshape((2,) * count + block.shape[1:])
    left = list(range(count))[::-1]
    me = lax.axis_index(axis)
    for bit in order:
        place = left.index(bit)
        left.pop(place)
        mine = (me >> bit) & 1
        kept = lax.dynamic_index_in_dim(block, mine, place, keepdims=False)
        sent = lax.dynamic_index_in_dim(block, 1 - mine, place, keepdims=False)
        got = swap_bit(sent, axis, bit)
        block = (kept.astype(jnp.float32) + got.astype(jnp.float32)).astype(block.dtype)
    return block


def double(block, axis, order):
    me = lax.axis_index(axis)
    seen = []
    for bit in order:
        got = swap_bit(block, axis, bit)
        low = ((me >> bit) & 1) == 0
        block = jnp.stack([jnp.where(low, block, got), jnp.where(low, got, block)])
        seen.insert(0, bit)
    count = len(order)
    want = list(range(count))[::-1]
    block = block.transpose([seen.index(bit) for bit in want] + list(range(count, block.ndim)))
    return block.reshape((2**count,) + block.shape[count:])


def total_over(block, axis):
    for bit in range(bits_of(axis)):
        block = block + swap_bit(block, axis, bit)
    return block


def to_heads(rows, parts):
    count = rows.shape[0]
    n = lax.axis_size(CTX)
    width = D // n
    stacked = rows.reshape(count, parts, n, width).transpose(2, 0, 1, 3).reshape(n, count, parts * width)
    moved = lax.all_to_all(stacked, CTX, split_axis=0, concat_axis=0, tiled=True)
    moved = moved.reshape(n * count, parts * width)
    return tuple(moved[:, p * width : (p + 1) * width] for p in range(parts))


def to_tokens(columns):
    parts = len(columns)
    n = lax.axis_size(CTX)
    total, width = columns[0].shape
    count = total // n
    joined = jnp.concatenate(columns, axis=1).reshape(n, count, parts * width)
    moved = lax.all_to_all(joined, CTX, split_axis=0, concat_axis=0, tiled=True)
    return moved.reshape(n, count, parts, width).transpose(1, 2, 0, 3).reshape(count, parts * n * width)


def layer_forward(stream, weights_now, position):
    (
        gain_one,
        shift_one,
        qkv_w,
        query_b,
        value_b,
        proj_w,
        proj_b,
        gain_two,
        shift_two,
        fc_w,
        fc_b,
        out_w,
        out_b,
    ) = weights_now
    normed_out, normed_one, inverse_one = layer_norm(
        stream, gain_one.astype(jnp.float32), shift_one.astype(jnp.float32)
    )
    attn_in = normed_out.astype(jnp.bfloat16)
    projected = jnp.dot(attn_in, qkv_w, preferred_element_type=jnp.float32)
    bias_row = jnp.concatenate([query_b, jnp.zeros_like(query_b), value_b]).astype(jnp.float32)
    qkv_rows = (projected + bias_row).astype(jnp.bfloat16)
    queries, key_rows, value_rows = to_heads(qkv_rows, 3)
    att_heads, lse_rows = run_attend(queries, key_rows, value_rows, position)
    att_out = to_tokens((att_heads,))
    middle = (
        stream
        + jnp.dot(att_out, proj_w, preferred_element_type=jnp.float32)
        + proj_b.astype(jnp.float32)
    )
    normed_mid, normed_two, inverse_two = layer_norm(
        middle, gain_two.astype(jnp.float32), shift_two.astype(jnp.float32)
    )
    mlp_in = normed_mid.astype(jnp.bfloat16)
    pre_act = jnp.dot(mlp_in, fc_w, preferred_element_type=jnp.float32) + fc_b.astype(jnp.float32)
    activated, gelu_slope = gelu_pair(pre_act)
    act_rows = activated.astype(jnp.bfloat16)
    result = (
        middle
        + jnp.dot(act_rows, out_w, preferred_element_type=jnp.float32)
        + out_b.astype(jnp.float32)
    )
    record = (
        normed_one,
        inverse_one,
        attn_in,
        queries,
        key_rows,
        value_rows,
        att_heads,
        att_out,
        lse_rows,
        normed_two,
        inverse_two,
        mlp_in,
        gelu_slope,
        act_rows,
    )
    return (result, record)


def layer_backward(upstream, weights_now, record, position):
    (
        gain_one,
        shift_one,
        qkv_w,
        query_b,
        value_b,
        proj_w,
        proj_b,
        gain_two,
        shift_two,
        fc_w,
        fc_b,
        out_w,
        out_b,
    ) = weights_now
    (
        normed_one,
        inverse_one,
        attn_in,
        queries,
        key_rows,
        value_rows,
        att_heads,
        att_out,
        lse_rows,
        normed_two,
        inverse_two,
        mlp_in,
        gelu_slope,
        act_rows,
    ) = record
    up_rows = upstream.astype(jnp.bfloat16)
    grad_out_b = jnp.sum(upstream, axis=0)
    grad_act = jnp.dot(up_rows, out_w.T, preferred_element_type=jnp.float32)
    grad_pre = grad_act * gelu_slope
    grad_pre_rows = grad_pre.astype(jnp.bfloat16)
    grad_fc_b = jnp.sum(grad_pre, axis=0)
    grad_mlp_in = jnp.dot(grad_pre_rows, fc_w.T, preferred_element_type=jnp.float32)
    back_two, grad_gain_two, grad_shift_two = norm_back(
        grad_mlp_in, normed_two, inverse_two, gain_two.astype(jnp.float32)
    )
    mid_grad = upstream + back_two
    mid_rows = mid_grad.astype(jnp.bfloat16)
    grad_proj_b = jnp.sum(mid_grad, axis=0)
    grad_att = jnp.dot(mid_rows, proj_w.T, preferred_element_type=jnp.float32).astype(jnp.bfloat16)
    (grad_heads,) = to_heads(grad_att, 1)
    grad_query, grad_key, grad_value = run_attend_back(
        queries, key_rows, value_rows, position, att_heads, grad_heads, lse_rows
    )
    head_sums = jnp.stack([jnp.sum(grad_query, axis=0), jnp.sum(grad_value, axis=0)])
    mine = lax.axis_index(CTX) * head_sums.shape[1]
    spread = lax.dynamic_update_slice(jnp.zeros((2, D), jnp.float32), head_sums, (0, mine))
    grad_query_b, grad_value_b = spread[0], spread[1]
    grad_qkv_rows = to_tokens(
        tuple(part.astype(jnp.bfloat16) for part in (grad_query, grad_key, grad_value))
    )
    grad_attn_in = jnp.dot(grad_qkv_rows, qkv_w.T, preferred_element_type=jnp.float32)
    back_one, grad_gain_one, grad_shift_one = norm_back(
        grad_attn_in, normed_one, inverse_one, gain_one.astype(jnp.float32)
    )
    new_upstream = mid_grad + back_one
    vectors = (
        grad_gain_one,
        grad_shift_one,
        grad_query_b,
        grad_value_b,
        grad_proj_b,
        grad_gain_two,
        grad_shift_two,
        grad_fc_b,
        grad_out_b,
    )
    row_pairs = (
        (attn_in, grad_qkv_rows),
        (att_out, mid_rows),
        (mlp_in, grad_pre_rows),
        (act_rows, up_rows),
    )
    return (new_upstream, vectors, row_pairs)


def assemble(vectors, matrices):
    return (
        vectors[0],
        vectors[1],
        matrices[0],
        vectors[2],
        vectors[3],
        matrices[1],
        vectors[4],
        vectors[5],
        vectors[6],
        matrices[2],
        vectors[7],
        matrices[3],
        vectors[8],
    )


def shards(
    tokens,
    cotangent,
    block_order,
    ln1_gain,
    ln1_bias,
    qkv_weight,
    query_bias,
    value_bias,
    proj_weight,
    proj_bias,
    ln2_gain,
    ln2_bias,
    fc_weight,
    fc_bias,
    out_weight,
    out_bias,
):
    row_count = tokens.shape[1]
    contexts = lax.axis_size(CTX)
    groups = lax.axis_size("fsdp")
    slots = block_order.shape[1]
    half_block = row_count * contexts // slots
    position = token_positions(block_order[0], row_count * contexts, half_block)
    stream = tokens[0].astype(jnp.float32)
    vectors_in = (
        ln1_gain, ln1_bias, query_bias, value_bias, proj_bias, ln2_gain, ln2_bias, fc_bias, out_bias,
    )
    sizes = [v.shape[1] for v in vectors_in]
    gathered = double(jnp.concatenate([v[0] for v in vectors_in])[None], "fsdp", list(range(bits_of("fsdp"))))
    gathered = gathered.reshape(groups, -1)
    gathered_vectors = []
    start = 0
    for size in sizes:
        gathered_vectors.append(gathered[:, start : start + size].reshape(groups * size))
        start += size
    me = lax.axis_index(CTX)

    def own_piece(weight):
        rows = weight.shape[1] // contexts
        return lax.dynamic_slice_in_dim(weight[0], me * rows, rows, axis=0)

    def gather_joined(pieces):
        return lax.all_gather(jnp.concatenate(pieces, axis=1), ("fsdp",) + CTX, axis=0, tiled=True)

    first = gather_joined((own_piece(qkv_weight), own_piece(proj_weight)))
    qkv_full, proj_full = first[:, : 3 * D], first[:, 3 * D :]
    fc_piece, out_piece = own_piece(fc_weight), own_piece(out_weight)
    rows = fc_piece.shape[0]
    quarters = out_piece.shape[0] // rows
    second = gather_joined(
        (fc_piece,) + tuple(out_piece[q * rows : (q + 1) * rows] for q in range(quarters))
    )
    hidden = fc_piece.shape[1]
    fc_full = second[:, :hidden]
    out_full = second[:, hidden:].reshape(groups * contexts, rows, quarters, D)
    out_full = out_full.transpose(0, 2, 1, 3).reshape(groups * contexts * rows * quarters, D)
    g = gathered_vectors
    full_weights = (
        g[0], g[1], qkv_full, g[2], g[3], proj_full, g[4], g[5], g[6], fc_full, g[7], out_full, g[8],
    )
    stream, record = layer_forward(stream, full_weights, position)
    upstream, vectors, row_pairs = layer_backward(cotangent[0], full_weights, record, position)
    z_bits = list(range(bits_of("fsdp")))
    chips = lax.axis_size("chip")
    core = lax.axis_index("core")
    matrices = [None] * 4
    for index in (3, 2, 1, 0):
        left, right = row_pairs[index]
        features = left.shape[1] // (groups * 2)
        pieces = left.reshape(row_count, groups, 2, features)
        pieces = pieces.transpose(2, 0, 1, 3).reshape(2, row_count, groups * features)
        own_half = lax.dynamic_index_in_dim(pieces, core, 0, keepdims=False)
        sent_half = lax.dynamic_index_in_dim(pieces, 1 - core, 0, keepdims=False)
        left_half = jnp.concatenate([own_half, swap_cores(sent_half)])
        right_pair = jnp.concatenate([right, swap_cores(right)])
        width = right.shape[1] // 2
        done = []
        for side in range(2):
            order = bit_order(side == 1)
            terms = dot_tn(left_half, right_pair[:, side * width : (side + 1) * width])
            terms = terms.astype(jnp.bfloat16).reshape(groups, chips, features // chips, width)
            terms = halve(terms.transpose(1, 0, 2, 3), "chip", order)
            part = halve(terms, "fsdp", z_bits[::-1])
            part = double(double(part, "chip", order), "core", [0])
            done.append(part.reshape(2 * features, width).astype(jnp.float32))
        matrices[index] = jnp.concatenate(done, axis=1)[None]
    packed = jnp.concatenate([v.reshape(groups, -1) for v in vectors], axis=1)
    packed = halve(packed, "fsdp", z_bits[::-1])
    own = total_over(total_over(packed, "core"), "chip")[None]
    vector_parts = []
    start = 0
    for v in vectors:
        size = v.shape[0] // groups
        vector_parts.append(own[:, start : start + size])
        start += size
    return (stream[None], upstream[None]) + assemble(vector_parts, matrices)


def solution(mesh):
    contexts, groups = mesh.devices.shape
    split_mesh = Mesh(mesh.devices.reshape(contexts // 2, 2, groups), ("chip", "core", "fsdp"))
    placed = (
        P("fsdp", CTX, None),
        P("fsdp", CTX, None),
        P("fsdp", None),
        P(None, "fsdp"),
        P(None, "fsdp"),
        P(None, "fsdp", None),
        P(None, "fsdp"),
        P(None, "fsdp"),
        P(None, "fsdp", None),
        P(None, "fsdp"),
        P(None, "fsdp"),
        P(None, "fsdp"),
        P(None, "fsdp", None),
        P(None, "fsdp"),
        P(None, "fsdp", None),
        P(None, "fsdp"),
    )
    return jax.shard_map(
        shards,
        mesh=split_mesh,
        in_specs=placed,
        out_specs=(
            P("fsdp", CTX, None),
            P("fsdp", CTX, None),
            P(None, "fsdp"),
            P(None, "fsdp"),
            P(None, "fsdp", None),
            P(None, "fsdp"),
            P(None, "fsdp"),
            P(None, "fsdp", None),
            P(None, "fsdp"),
            P(None, "fsdp"),
            P(None, "fsdp"),
            P(None, "fsdp", None),
            P(None, "fsdp"),
            P(None, "fsdp", None),
            P(None, "fsdp"),
        ),
        check_vma=False,
    )
```
